32 devices in a mesh: camp: 4 (over y, core), hour: 8 (over z, x).
Axes of the slice: x: 2, y: 2, z: 4, core: 2. Of those that a mesh axis runs over, the one named last changes fastest.
Arguments:
- observed: bfloat16 [512, 1024, 128], P('camp', 'hour'), may hold values from -6 to 6
- bucket: int32 [512, 1024, 128], P('camp', 'hour'), may hold values from 0 to 8
- propensity: float32 [8], replicated, may hold values from 0.1 to 1
- camp_factor: float32 [512, 256], P(('camp', 'hour')), may hold values from -2.4 to 2.4
- camp_moment: float32 [512, 256], P(('camp', 'hour')), may hold values from -0.6 to 0.6
- camp_second: float32 [512, 256], P(('camp', 'hour')), may hold values from 0.02 to 0.5
- hour_factor: float32 [1024, 256], P(('hour', 'camp')), may hold values from -2.4 to 2.4
- hour_moment: float32 [1024, 256], P(('hour', 'camp')), may hold values from -0.6 to 0.6
- hour_second: float32 [1024, 256], P(('hour', 'camp')), may hold values from 0.02 to 0.5
- delay_factor: float32 [128, 256], replicated, may hold values from -2.4 to 2.4
- delay_moment: float32 [128, 256], replicated, may hold values from -0.6 to 0.6
- delay_second: float32 [128, 256], replicated, may hold values from 0.02 to 0.5
Outputs:
- new_camp: float32 [512, 256], P(('camp', 'hour'))
- new_hour: float32 [1024, 256], P(('hour', 'camp'))
- new_delay: float32 [128, 256], replicated
The draws below stay inside these ranges and needn't reach their ends.
Inputs may be any that keep to these rules, and one draw needn't show every extreme that they name: 0 marks a censored entry; bucket b of 1 to 8 takes propensity entry b - 1.
All inputs are finite; a program needn't handle non-finite values.
Results may differ from the reference program's by a relative error of at most 0.01.
Values may be sent and summed in bfloat16 or wider, within the bound.
No kernel may reach another device: no remote copies, remote signals or barrier semaphores. Data moves between devices by JAX's collectives and lax.ppermute only.
A program may use at most 128 MiB of HBM per device.

```python
import math
import jax
import jax.numpy as jnp
from jax import lax

RANK = 256
DELAYS = 128
LEVELS = 8
STEPS = 2
CAMP_DEV = 128
CAMPAIGNS = 512
HOURS = 1024


def touch_ends(drawn, stream_key, least, largest):
    longest = drawn.shape.index(max(drawn.shape))
    spots = []
    for shift in (0, 1):
        where = [jax.random.randint(jax.random.fold_in(stream_key, axis), (), 0, length) for axis, length in enumerate(drawn.shape)]
        where[longest] = (where[longest] + shift) % drawn.shape[longest]
        spots.append(tuple(where))
    return drawn.at[spots[0]].set(least).at[spots[1]].set(largest)


def block_levels(own_key, shape, cuts, least, largest):
    def one(axis_at, blocks):
        steps = jax.random.uniform(jax.random.fold_in(jax.random.fold_in(own_key, 6), axis_at), (blocks,), jnp.float32, least / len(cuts), largest / len(cuts))
        return jnp.repeat(jnp.exp(steps), shape[axis_at] // blocks).reshape((-1,) + (1,) * (len(shape) - axis_at - 1))

    level = one(*cuts[0])
    for cut in cuts[1:]:
        level = level * one(*cut)
    return level


def centred(rng, shape, width, bound, cuts=(), kind=jnp.bfloat16):
    entries = jax.random.normal(rng, shape, jnp.float32) * width
    if len(cuts) > 0:
        entries = block_levels(rng, shape, cuts, -0.22, 0.18) * entries
    return jnp.clip(entries, min=-bound, max=bound).astype(kind)


def setup_inputs(seed: int = 0) -> dict:
    keys = jax.random.split(jax.random.key(seed), 13)
    observed = centred(keys[0], (CAMPAIGNS, HOURS, DELAYS), 1.0, 6.0, ((0, 4), (1, 8)))
    bucket = touch_ends(jax.random.randint(keys[1], (CAMPAIGNS, HOURS, DELAYS), 0, LEVELS + 1), jax.random.fold_in(keys[1], 1), 0, LEVELS).astype(jnp.int32)
    propensity = jnp.clip(jnp.exp(jax.random.uniform(keys[2], (LEVELS,), jnp.float32, math.log(0.1), math.log(1.0))), 0.1, 1.0)
    camp_factor = centred(keys[3], (CAMPAIGNS, RANK), 0.4, 2.4, ((0, 32),), jnp.float32)
    camp_moment = centred(keys[4], (CAMPAIGNS, RANK), 0.1, 0.6, ((0, 32),), jnp.float32)
    camp_second = jnp.clip(jnp.exp(math.log(0.5) - 3.218876 * jax.random.uniform(keys[5], (CAMPAIGNS, RANK), jnp.float32) ** block_levels(keys[5], (CAMPAIGNS, RANK), ((0, 32),), -0.2, 0.2)), 0.02, 0.5)
    hour_factor = centred(keys[6], (HOURS, RANK), 0.4, 2.4, ((0, 32),), jnp.float32)
    hour_moment = centred(keys[7], (HOURS, RANK), 0.1, 0.6, ((0, 32),), jnp.float32)
    hour_second = jnp.clip(jnp.exp(math.log(0.5) - 3.218876 * jax.random.uniform(keys[8], (HOURS, RANK), jnp.float32) ** block_levels(keys[8], (HOURS, RANK), ((0, 32),), -0.2, 0.2)), 0.02, 0.5)
    delay_factor = centred(keys[9], (DELAYS, RANK), 0.4, 2.4, (), jnp.float32)
    delay_moment = centred(keys[10], (DELAYS, RANK), 0.1, 0.6, (), jnp.float32)
    delay_second = jnp.clip(jnp.exp(jax.random.uniform(keys[11], (DELAYS, RANK), jnp.float32, math.log(0.02), math.log(0.5))), 0.02, 0.5)
    return dict(observed=observed, bucket=bucket, propensity=propensity, camp_factor=camp_factor, camp_moment=camp_moment, camp_second=camp_second, hour_factor=hour_factor, hour_moment=hour_moment, hour_second=hour_second, delay_factor=delay_factor, delay_moment=delay_moment, delay_second=delay_second)


learn_rate = 0.1
beta_first = 0.9
beta_second = 0.999
adam_eps = 1e-08

def adam_update(factor, moment, second, gradient, grad_scale):
    scaled = gradient * grad_scale
    moment = beta_first * moment + (1.0 - beta_first) * scaled
    second = beta_second * second + (1.0 - beta_second) * scaled * scaled
    factor = factor - learn_rate * moment / (jnp.sqrt(second) + adam_eps)
    return (factor, moment, second)

def gradients(observed, bucket, inverse, camp_factor, hour_factor, delay_factor):
    camp_block = camp_factor.astype(jnp.bfloat16)
    hour_block = hour_factor.astype(jnp.bfloat16)
    delay_block = delay_factor.astype(jnp.bfloat16)
    khatri = (hour_block.astype(jnp.float32)[:, None, :] * delay_block.astype(jnp.float32)[None, :, :]).astype(jnp.bfloat16)
    khatri = khatri.reshape(HOURS * DELAYS, RANK)
    slabs = CAMPAIGNS // CAMP_DEV
    observed_slabs = observed.reshape(slabs, CAMP_DEV, HOURS * DELAYS)
    bucket_slabs = bucket.reshape(slabs, CAMP_DEV, HOURS * DELAYS)
    camp_slabs = camp_block.reshape(slabs, CAMP_DEV, RANK)

    def visit(totals, slab_item):
        obs_slab, bucket_slab, camp_slab = slab_item
        picked = inverse[jnp.clip(bucket_slab - 1, 0, LEVELS - 1).astype(jnp.int32)]
        weight = jnp.where(bucket_slab > 0, picked, jnp.zeros_like(picked))
        model_tile = lax.dot_general(camp_slab, khatri, (((1,), (1,)), ((), ())), preferred_element_type=jnp.float32)
        residual = (weight * (model_tile - obs_slab.astype(jnp.float32))).astype(jnp.bfloat16)
        camp_grad = jnp.dot(residual, khatri, preferred_element_type=jnp.float32)
        spread = lax.dot_general(residual, camp_slab, (((0,), (0,)), ((), ())), preferred_element_type=jnp.float32)
        spread = spread.reshape(HOURS, DELAYS, RANK)
        hour_total = totals[0] + lax.optimization_barrier(jnp.sum(spread * delay_block.astype(jnp.float32)[None, :, :], axis=1))
        delay_total = totals[1] + lax.optimization_barrier(jnp.sum(spread * hour_block.astype(jnp.float32)[:, None, :], axis=0))
        return ((hour_total, delay_total), camp_grad)
    start = (jnp.zeros((HOURS, RANK), jnp.float32), jnp.zeros((DELAYS, RANK), jnp.float32))
    (hour_grad, delay_grad), camp_grads = lax.scan(visit, start, (observed_slabs, bucket_slabs, camp_slabs))
    return (camp_grads.reshape(CAMPAIGNS, RANK), hour_grad, delay_grad)

def reference(observed, bucket, propensity, camp_factor, camp_moment, camp_second, hour_factor, hour_moment, hour_second, delay_factor, delay_moment, delay_second):
    inverse = 1.0 / propensity
    camp_scale = 1.0 / math.sqrt(HOURS * DELAYS)
    hour_scale = 1.0 / math.sqrt(CAMPAIGNS * DELAYS)
    delay_scale = 1.0 / math.sqrt(CAMPAIGNS * HOURS)
    for iteration in range(STEPS):
        camp_grad, hour_grad, delay_grad = gradients(observed, bucket, inverse, camp_factor, hour_factor, delay_factor)
        camp_factor, camp_moment, camp_second = adam_update(camp_factor, camp_moment, camp_second, camp_grad, camp_scale)
        hour_factor, hour_moment, hour_second = adam_update(hour_factor, hour_moment, hour_second, hour_grad, hour_scale)
        delay_factor, delay_moment, delay_second = adam_update(delay_factor, delay_moment, delay_second, delay_grad, delay_scale)
    return (camp_factor, hour_factor, delay_factor)
```

```python
import math

import jax
import jax.numpy as jnp
from jax import lax
from jax.experimental import pallas as pl
from jax.experimental.pallas import tpu as pltpu
from jax.sharding import PartitionSpec as P

learn_rate = 0.1
beta_first = 0.9
beta_second = 0.999
adam_eps = 1e-08

F32 = jnp.float32
BF16 = jnp.bfloat16


def adam_update(factor, moment, second, gradient, grad_scale):
    scaled = gradient * grad_scale
    moment = beta_first * moment + (1.0 - beta_first) * scaled
    second = beta_second * second + (1.0 - beta_second) * scaled * scaled
    factor = factor - learn_rate * moment / (jnp.sqrt(second) + adam_eps)
    return (factor, moment, second)


def grads_kernel(prop_ref, obs_ref, bucket_ref, camp_ref, hour_ref, delay_ref, ga_ref, gb_ref, gc_ref, gb_sum, gc_sum):
    step = pl.program_id(0)
    rows, cols, delays = obs_ref.shape
    rank = hour_ref.shape[1]
    levels = prop_ref.shape[0]
    flat = rows * cols

    @pl.when(step == 0)
    def _():
        gb_sum[...] = jnp.zeros_like(gb_sum)
        gc_sum[...] = jnp.zeros_like(gc_sum)

    lane = lax.broadcasted_iota(jnp.int32, (8, delays), 1)
    chance = jnp.ones((8, delays), F32)
    for level in range(levels):
        chance = jnp.where(lane == level + 1, prop_ref[level], chance)
    table = jnp.where(lane == 0, 0.0, 1.0 / chance)
    table = jnp.broadcast_to(table[:1], (flat, delays))
    weight = jnp.take_along_axis(table, bucket_ref[...].reshape(flat, delays), axis=1)

    camp = camp_ref[...]
    hour = hour_ref[...]
    delay = delay_ref[...]
    pair = (camp[:, None, :] * hour[None, :, :]).reshape(flat, rank)
    model = lax.dot_general(pair, delay, (((1,), (1,)), ((), ())), preferred_element_type=F32)
    observed = obs_ref[...].reshape(flat, delays).astype(F32)
    residual = (weight * (model - observed)).astype(BF16)
    back = lax.dot_general(residual, delay, (((1,), (0,)), ((), ())), preferred_element_type=F32)
    back = back.reshape(rows, cols, rank)
    ga_ref[...] = jnp.sum(back * hour.astype(F32)[None, :, :], axis=1).astype(ga_ref.dtype)
    gb_sum[...] += jnp.sum(back * camp.astype(F32)[:, None, :], axis=0)
    gc_sum[...] += lax.dot_general(residual, pair, (((0,), (0,)), ((), ())), preferred_element_type=F32)

    @pl.when(step == pl.num_programs(0) - 1)
    def _():
        gb_ref[...] = gb_sum[...].astype(gb_ref.dtype)
        gc_ref[...] = gc_sum[...].astype(gc_ref.dtype)


def gradients(propensity, observed, bucket, camp_block, hour_block, delay_block):
    tile_rows, tile_cols, delay_count = observed.shape
    rank = camp_block.shape[1]
    rows = math.gcd(tile_rows, 16)

    def whole(shape):
        return pl.BlockSpec(shape, lambda i: (0,) * len(shape))

    tile = pl.BlockSpec((rows, tile_cols, delay_count), lambda i: (i, 0, 0))
    strip = pl.BlockSpec((rows, rank), lambda i: (i, 0))
    return pl.pallas_call(
        grads_kernel,
        grid=(tile_rows // rows,),
        in_specs=[
            pl.BlockSpec(memory_space=pltpu.SMEM),
            tile,
            tile,
            strip,
            whole((tile_cols, rank)),
            whole((delay_count, rank)),
        ],
        out_specs=[strip, whole((tile_cols, rank)), whole((delay_count, rank))],
        out_shape=[
            jax.ShapeDtypeStruct((tile_rows, rank), BF16),
            jax.ShapeDtypeStruct((tile_cols, rank), BF16),
            jax.ShapeDtypeStruct((delay_count, rank), BF16),
        ],
        scratch_shapes=[pltpu.VMEM((tile_cols, rank), F32), pltpu.VMEM((delay_count, rank), F32)],
        compiler_params=pltpu.CompilerParams(vmem_limit_bytes=48 * 1024 * 1024),
        cost_estimate=pl.CostEstimate(
            flops=6 * tile_rows * tile_cols * delay_count * rank,
            bytes_accessed=6 * tile_rows * tile_cols * delay_count,
            transcendentals=0,
        ),
        name="gradients",
    )(propensity, observed, bucket, camp_block, hour_block, delay_block)


def swap(block, axis, bit):
    size = lax.axis_size(axis)
    return lax.ppermute(block, axis, [(i, i ^ bit) for i in range(size)])


def bits_of(axis):
    size = lax.axis_size(axis)
    assert size & (size - 1) == 0
    return [1 << n for n in range(size.bit_length() - 1)]


def gather_blocks(block, axis):
    index = lax.axis_index(axis)
    for depth, bit in enumerate(reversed(bits_of(axis))):
        other = swap(block, axis, bit)
        high = (index & bit) != 0
        low_block = jnp.where(high, other, block)
        high_block = jnp.where(high, block, other)
        block = jnp.stack([low_block, high_block], axis=depth)
    count = lax.axis_size(axis)
    return block.reshape((count,) + block.shape[len(bits_of(axis)):])


def sum_step(block, axis, bit):
    total = block.astype(F32) + swap(block, axis, bit).astype(F32)
    return lax.optimization_barrier(total.astype(BF16))


def sum_all(camp_grad, hour_grad, delay_grad):
    cols = hour_grad.shape[0]
    rows = camp_grad.shape[0]
    joint = jnp.concatenate([hour_grad, delay_grad])
    for bit in bits_of("camp"):
        joint = sum_step(joint, "camp", bit)
    hour_sum, delay_part = joint[:cols], joint[cols:]
    joint = jnp.concatenate([camp_grad, delay_part])
    for bit in bits_of("hour"):
        joint = sum_step(joint, "hour", bit)
    return joint[:rows], hour_sum, joint[rows:]


def pack(factor, moment, second):
    high = factor.astype(BF16)
    return jnp.stack([high, moment.astype(BF16), second.astype(BF16)])


def own_rows(block, axis, count):
    return lax.dynamic_slice_in_dim(block, lax.axis_index(axis) * count, count, 0)


def body(
    observed,
    bucket,
    propensity,
    camp_factor,
    camp_moment,
    camp_second,
    hour_factor,
    hour_moment,
    hour_second,
    delay_factor,
    delay_moment,
    delay_second,
):
    tile_rows, tile_cols, delay_count = observed.shape
    camp_own, hour_own = camp_factor.shape[0], hour_factor.shape[0]
    campaigns = tile_rows * lax.axis_size("camp")
    total_hours = tile_cols * lax.axis_size("hour")
    rank = camp_factor.shape[1]
    camp_scale = 1.0 / math.sqrt(total_hours * delay_count)
    hour_scale = 1.0 / math.sqrt(campaigns * delay_count)
    delay_scale = 1.0 / math.sqrt(campaigns * total_hours)

    camp_all = gather_blocks(pack(camp_factor, camp_moment, camp_second), "hour")
    hour_all = gather_blocks(pack(hour_factor, hour_moment, hour_second), "camp")
    camp_all = [camp_all[:, n].reshape(tile_rows, rank) for n in range(3)]
    hour_all = [hour_all[:, n].reshape(tile_cols, rank) for n in range(3)]
    camp_block, hour_block, delay_block = camp_all[0], hour_all[0], delay_factor.astype(BF16)

    partial = gradients(propensity, observed, bucket, camp_block, hour_block, delay_block)
    camp_grad, hour_grad, delay_grad = (g.astype(F32) for g in sum_all(*partial))
    camp_block = adam_update(*(x.astype(F32) for x in camp_all), camp_grad, camp_scale)[0].astype(BF16)
    hour_block = adam_update(*(x.astype(F32) for x in hour_all), hour_grad, hour_scale)[0].astype(BF16)
    camp_state = adam_update(
        camp_factor, camp_moment, camp_second, own_rows(camp_grad, "hour", camp_own), camp_scale
    )
    hour_state = adam_update(
        hour_factor, hour_moment, hour_second, own_rows(hour_grad, "camp", hour_own), hour_scale
    )
    delay_state = adam_update(delay_factor, delay_moment, delay_second, delay_grad, delay_scale)
    delay_block = delay_state[0].astype(BF16)

    partial = gradients(propensity, observed, bucket, camp_block, hour_block, delay_block)
    camp_grad, hour_grad, delay_grad = (g.astype(F32) for g in sum_all(*partial))
    camp_new = adam_update(*camp_state, own_rows(camp_grad, "hour", camp_own), camp_scale)[0]
    hour_new = adam_update(*hour_state, own_rows(hour_grad, "camp", hour_own), hour_scale)[0]
    delay_new = adam_update(*delay_state, delay_grad, delay_scale)[0]
    return (camp_new, hour_new, delay_new)


def solution(mesh):
    in_specs = (
        P("camp", "hour", None),
        P("camp", "hour", None),
        P(),
        P(("camp", "hour"), None),
        P(("camp", "hour"), None),
        P(("camp", "hour"), None),
        P(("hour", "camp"), None),
        P(("hour", "camp"), None),
        P(("hour", "camp"), None),
        P(),
        P(),
        P(),
    )
    out_specs = (P(("camp", "hour"), None), P(("hour", "camp"), None), P())
    return jax.shard_map(body, mesh=mesh, in_specs=in_specs, out_specs=out_specs, check_vma=False)
```

```python
import math

import jax
import jax.numpy as jnp
from jax import lax
from jax.experimental import pallas as pl
from jax.experimental.pallas import tpu as pltpu
from jax.sharding import PartitionSpec as P

learn_rate = 0.1
beta_first = 0.9
beta_second = 0.999
adam_eps = 1e-08

F32 = jnp.float32
BF16 = jnp.bfloat16


def adam_update(factor, moment, second, gradient, grad_scale):
    scaled = gradient * grad_scale
    moment = beta_first * moment + (1.0 - beta_first) * scaled
    second = beta_second * second + (1.0 - beta_second) * scaled * scaled
    factor = factor - learn_rate * moment / (jnp.sqrt(second) + adam_eps)
    return (factor, moment, second)


def grads_kernel(
    prop_ref, obs_hbm, bucket_hbm, camp_ref, hour_ref, delay_ref,
    ga_ref, gb_ref, gc_ref, gb_sum, gc_sum, obs_ref, bucket_ref, sems,
):
    total, cols, delays = obs_ref.shape
    rank = hour_ref.shape[1]
    parts = sems.shape[1]
    rows = total // parts
    sub = math.gcd(rows, 8)
    flat = sub * cols

    def fetches(part):
        at = pl.ds(part * rows, rows)
        return (
            pltpu.make_async_copy(obs_hbm.at[at], obs_ref.at[at], sems.at[0, part]),
            pltpu.make_async_copy(bucket_hbm.at[at], bucket_ref.at[at], sems.at[1, part]),
        )

    for part in range(parts):
        for fetch in fetches(part):
            fetch.start()

    gb_sum[...] = jnp.zeros_like(gb_sum)
    gc_sum[...] = jnp.zeros_like(gc_sum)
    lane = lax.broadcasted_iota(jnp.int32, (8, delays), 1)
    chance = jnp.ones((8, delays), F32)
    for level in range(prop_ref.shape[0]):
        chance = jnp.where(lane == level + 1, prop_ref[level], chance)
    table = jnp.where(lane == 0, 0.0, 1.0 / chance)
    table = jnp.broadcast_to(table[:1], (flat, delays))

    hour16 = hour_ref[...]
    hour = hour16.astype(F32)
    delay = delay_ref[...]

    for part in range(parts):
        for fetch in fetches(part):
            fetch.wait()
        gb_part, gc_part = gb_sum[...], gc_sum[...]
        for start in range(part * rows, (part + 1) * rows, sub):
            camp = camp_ref[start:start + sub]
            pair = (camp[:, None, :] * hour16[None, :, :]).reshape(flat, rank)
            model = lax.dot_general(pair, delay, (((1,), (1,)), ((), ())), preferred_element_type=F32)
            bucket = bucket_ref[start:start + sub].reshape(flat, delays)
            weight = jnp.take_along_axis(table, bucket, axis=1)
            observed = obs_ref[start:start + sub].reshape(flat, delays).astype(F32)
            residual = (weight * (model - observed)).astype(BF16)
            back = jnp.dot(residual, delay, preferred_element_type=F32).reshape(sub, cols, rank)
            ga_ref[start:start + sub] = jnp.sum(back * hour[None, :, :], axis=1)
            gb_part += jnp.sum(back * camp.astype(F32)[:, None, :], axis=0)
            gc_part += lax.dot_general(residual, pair, (((0,), (0,)), ((), ())), preferred_element_type=F32)
        gb_sum[...] = gb_part
        gc_sum[...] = gc_part
    gb_ref[...] = gb_sum[...].astype(gb_ref.dtype)
    gc_ref[...] = gc_sum[...].astype(gc_ref.dtype)


def gradients(propensity, observed, bucket, camp_block, hour_block, delay_block):
    tile_rows, tile_cols, delay_count = observed.shape
    rank = camp_block.shape[1]
    parts = tile_rows // math.gcd(tile_rows, 16)
    vmem = pl.BlockSpec(memory_space=pltpu.VMEM)
    hbm = pl.BlockSpec(memory_space=pltpu.HBM)
    observed, bucket = (pltpu.with_memory_space_constraint(x, pltpu.HBM) for x in (observed, bucket))
    return pl.pallas_call(
        grads_kernel,
        in_specs=[pl.BlockSpec(memory_space=pltpu.SMEM), hbm, hbm, vmem, vmem, vmem],
        out_specs=[vmem, vmem, vmem],
        out_shape=[
            jax.ShapeDtypeStruct((tile_rows, rank), F32),
            jax.ShapeDtypeStruct((tile_cols, rank), BF16),
            jax.ShapeDtypeStruct((delay_count, rank), BF16),
        ],
        scratch_shapes=[
            pltpu.VMEM((tile_cols, rank), F32),
            pltpu.VMEM((delay_count, rank), F32),
            pltpu.VMEM(observed.shape, observed.dtype),
            pltpu.VMEM(bucket.shape, bucket.dtype),
            pltpu.SemaphoreType.DMA((2, parts)),
        ],
        compiler_params=pltpu.CompilerParams(vmem_limit_bytes=40 * 1024 * 1024),
        cost_estimate=pl.CostEstimate(
            flops=6 * tile_rows * tile_cols * delay_count * rank,
            bytes_accessed=6 * tile_rows * tile_cols * delay_count,
            transcendentals=0,
        ),
        name="gradients",
    )(propensity, observed, bucket, camp_block, hour_block, delay_block)


def pack_kernel(*refs):
    camp, hour, delay, camp_out, hour_out, delay_out = refs[:3], refs[3:6], refs[6], *refs[7:]
    for n in range(3):
        camp_out[n] = camp[n][...].astype(BF16)
        hour_out[n] = hour[n][...].astype(BF16)
    delay_out[...] = delay[...].astype(BF16)


def pack(camp, hour, delay):
    vmem = pl.BlockSpec(memory_space=pltpu.VMEM)
    return pl.pallas_call(
        pack_kernel,
        in_specs=[vmem] * 7,
        out_specs=[vmem] * 3,
        out_shape=[
            jax.ShapeDtypeStruct((3,) + camp[0].shape, BF16),
            jax.ShapeDtypeStruct((3,) + hour[0].shape, BF16),
            jax.ShapeDtypeStruct(delay.shape, BF16),
        ],
        name="pack",
    )(*camp, *hour, delay)


def swap(block, axis, bit):
    size = lax.axis_size(axis)
    return lax.ppermute(block, axis, [(i, i ^ bit) for i in range(size)])


def bits_of(axis):
    size = lax.axis_size(axis)
    assert size & (size - 1) == 0
    return [1 << n for n in range(size.bit_length() - 1)]


def gather_blocks(block, axis):
    index = lax.axis_index(axis)
    for depth, bit in enumerate(reversed(bits_of(axis))):
        other = swap(block, axis, bit)
        high = (index & bit) != 0
        low_block = jnp.where(high, other, block)
        high_block = jnp.where(high, block, other)
        block = jnp.stack([low_block, high_block], axis=depth)
    count = lax.axis_size(axis)
    return block.reshape((count,) + block.shape[len(bits_of(axis)):])


def swap_both(block, camp_bit, hour_bit):
    hours = lax.axis_size("hour")
    size = lax.axis_size("camp") * hours
    return lax.ppermute(block, ("camp", "hour"), [(i, i ^ (camp_bit * hours + hour_bit)) for i in range(size)])


def add(*terms):
    terms = [t.astype(F32) for t in terms]
    while len(terms) > 1:
        terms = [terms[n] + terms[n + 1] for n in range(0, len(terms), 2)]
    return terms[0]


def rounded(block):
    return lax.optimization_barrier(block.astype(BF16))


class Rows:
    def __init__(self, block, axis, whole):
        self.axis, self.whole, self.bits = axis, whole, bits_of(axis)[::-1]
        self.block = block
        if not whole:
            rows, rank = block.shape
            own = rows >> len(self.bits)
            self.block = block.reshape((2,) * len(self.bits) + (own, rank))

    def send(self, bit):
        if self.whole:
            return self.block
        at = self.bits.index(bit)
        low, high = (lax.index_in_dim(self.block, n, at, keepdims=False) for n in (0, 1))
        is_high = (lax.axis_index(self.axis) & bit) != 0
        self.block = jnp.where(is_high, high, low)
        self.bits.remove(bit)
        return jnp.where(is_high, low, high)

    def receive(self, other):
        self.block = rounded(add(self.block, other))


def exchange(gradient, bit, extra):
    sent = gradient.send(bit)
    rank = sent.shape[-1]
    joint = jnp.concatenate([sent.reshape(-1, rank), extra])
    joint = swap(joint, gradient.axis, bit)
    gradient.receive(joint[:-extra.shape[0]].reshape(sent.shape))
    return joint[-extra.shape[0]:]


def sum_all(camp_grad, hour_grad, delay_grad, whole):
    camp_bits, hour_bits = bits_of("camp"), bits_of("hour")
    camp_rows = Rows(camp_grad.astype(BF16), "hour", whole)
    hour_rows = Rows(hour_grad, "camp", whole)
    first = camp_bits.pop(0)
    half = delay_grad.shape[0] // 2
    is_high = (lax.axis_index("camp") & first) != 0
    low, high = delay_grad[:half], delay_grad[half:]
    kept = jnp.where(is_high, high, low)
    delay_part = rounded(add(kept, exchange(hour_rows, first, jnp.where(is_high, low, high))))
    while camp_bits and hour_bits:
        camp_bit, hour_bit = camp_bits.pop(0), hour_bits.pop(0)
        other_camp = exchange(hour_rows, camp_bit, delay_part)
        other_hour = exchange(camp_rows, hour_bit, delay_part)
        other_both = swap_both(delay_part, camp_bit, hour_bit)
        delay_part = rounded(add(delay_part, other_hour, other_camp, other_both))
    for rows, bits in ((hour_rows, camp_bits), (camp_rows, hour_bits)):
        for bit in bits:
            delay_part = rounded(add(delay_part, exchange(rows, bit, delay_part)))
    other = swap(delay_part, "camp", first)
    delay_sum = jnp.concatenate([jnp.where(is_high, other, delay_part), jnp.where(is_high, delay_part, other)])
    return camp_rows.block.astype(F32), hour_rows.block.astype(F32), delay_sum.astype(F32)


def own_rows(block, axis, count):
    return lax.dynamic_slice_in_dim(block, lax.axis_index(axis) * count, count, 0)


def body(
    observed,
    bucket,
    propensity,
    camp_factor,
    camp_moment,
    camp_second,
    hour_factor,
    hour_moment,
    hour_second,
    delay_factor,
    delay_moment,
    delay_second,
):
    tile_rows, tile_cols, delay_count = observed.shape
    camp_own, hour_own = camp_factor.shape[0], hour_factor.shape[0]
    campaigns = tile_rows * lax.axis_size("camp")
    total_hours = tile_cols * lax.axis_size("hour")
    rank = camp_factor.shape[1]
    camp_scale = 1.0 / math.sqrt(total_hours * delay_count)
    hour_scale = 1.0 / math.sqrt(campaigns * delay_count)
    delay_scale = 1.0 / math.sqrt(campaigns * total_hours)

    camp_state = (camp_factor, camp_moment, camp_second)
    hour_state = (hour_factor, hour_moment, hour_second)
    camp_packed, hour_packed, delay_block = pack(camp_state, hour_state, delay_factor)
    camp_all = gather_blocks(camp_packed, "hour")
    hour_all = gather_blocks(hour_packed, "camp")
    camp_all = [camp_all[:, n].reshape(tile_rows, rank) for n in range(3)]
    hour_all = [hour_all[:, n].reshape(tile_cols, rank) for n in range(3)]
    camp_block, hour_block = camp_all[0], hour_all[0]

    partial = gradients(propensity, observed, bucket, camp_block, hour_block, delay_block)
    camp_grad, hour_grad, delay_grad = sum_all(*partial, whole=True)
    camp_block = adam_update(*(x.astype(F32) for x in camp_all), camp_grad, camp_scale)[0].astype(BF16)
    hour_block = adam_update(*(x.astype(F32) for x in hour_all), hour_grad, hour_scale)[0].astype(BF16)
    camp_state = adam_update(*camp_state, own_rows(camp_grad, "hour", camp_own), camp_scale)
    hour_state = adam_update(*hour_state, own_rows(hour_grad, "camp", hour_own), hour_scale)
    delay_state = adam_update(delay_factor, delay_moment, delay_second, delay_grad, delay_scale)
    delay_block = delay_state[0].astype(BF16)

    partial = gradients(propensity, observed, bucket, camp_block, hour_block, delay_block)
    camp_grad, hour_grad, delay_grad = sum_all(*partial, whole=False)
    camp_new = adam_update(*camp_state, camp_grad, camp_scale)[0]
    hour_new = adam_update(*hour_state, hour_grad, hour_scale)[0]
    delay_new = adam_update(*delay_state, delay_grad, delay_scale)[0]
    return (camp_new, hour_new, delay_new)


def solution(mesh):
    in_specs = (
        P("camp", "hour", None),
        P("camp", "hour", None),
        P(),
        P(("camp", "hour"), None),
        P(("camp", "hour"), None),
        P(("camp", "hour"), None),
        P(("hour", "camp"), None),
        P(("hour", "camp"), None),
        P(("hour", "camp"), None),
        P(),
        P(),
        P(),
    )
    out_specs = (P(("camp", "hour"), None), P(("hour", "camp"), None), P())
    return jax.shard_map(body, mesh=mesh, in_specs=in_specs, out_specs=out_specs, check_vma=False)
```

```python
import math

import jax
import jax.numpy as jnp
from jax import lax
from jax.experimental import pallas as pl
from jax.experimental.pallas import tpu as pltpu
from jax.sharding import PartitionSpec as P

learn_rate = 0.1
beta_first = 0.9
beta_second = 0.999
adam_eps = 1e-08

F32 = jnp.float32
BF16 = jnp.bfloat16


def adam_update(factor, moment, second, gradient, grad_scale):
    scaled = gradient * grad_scale
    moment = beta_first * moment + (1.0 - beta_first) * scaled
    second = beta_second * second + (1.0 - beta_second) * scaled * scaled
    factor = factor - learn_rate * moment / (jnp.sqrt(second) + adam_eps)
    return (factor, moment, second)


def fill_table(table_ref, prop_ref):
    lane = lax.broadcasted_iota(jnp.int32, table_ref.shape, 1)
    chance = jnp.ones(table_ref.shape, F32)
    for level in range(prop_ref.shape[0]):
        chance = jnp.where(lane == level + 1, prop_ref[level], chance)
    table_ref[...] = jnp.where(lane == 0, 0.0, 1.0 / chance)


def tile_gradients(
    table_ref, obs_ref, bucket_ref, camp_ref, hour_ref, delay_ref,
    ga_ref, gb_ref, gc_ref, gb_sum, gc_sum, parts, arrived,
):
    total, cols, delays = obs_ref.shape
    rank = hour_ref.shape[1]
    rows = total // parts
    sub = math.gcd(rows, 8)
    flat = sub * cols
    gb_sum[...] = jnp.zeros_like(gb_sum)
    gc_sum[...] = jnp.zeros_like(gc_sum)
    hour16 = hour_ref[...]
    hour = hour16.astype(F32)
    delay = delay_ref[...]
    for part in range(parts):
        arrived(part)
        table = jnp.broadcast_to(table_ref[:1], (flat, delays))
        gb_part, gc_part = gb_sum[...], gc_sum[...]
        for start in range(part * rows, (part + 1) * rows, sub):
            camp = camp_ref[start:start + sub]
            pair = (camp[:, None, :] * hour16[None, :, :]).reshape(flat, rank)
            model = lax.dot_general(pair, delay, (((1,), (1,)), ((), ())), preferred_element_type=F32)
            bucket = bucket_ref[start:start + sub].reshape(flat, delays)
            weight = jnp.take_along_axis(table, bucket, axis=1)
            observed = obs_ref[start:start + sub].reshape(flat, delays).astype(F32)
            residual = (weight * (model - observed)).astype(BF16)
            back = jnp.dot(residual, delay, preferred_element_type=F32).reshape(sub, cols, rank)
            ga_ref[start:start + sub] = jnp.sum(back * hour[None, :, :], axis=1)
            gb_part += jnp.sum(back * camp.astype(F32)[:, None, :], axis=0)
            gc_part += lax.dot_general(residual, pair, (((0,), (0,)), ((), ())), preferred_element_type=F32)
        gb_sum[...] = gb_part
        gc_sum[...] = gc_part
    gb_ref[...] = gb_sum[...].astype(gb_ref.dtype)
    gc_ref[...] = gc_sum[...].astype(gc_ref.dtype)


AHEAD = 3


def grads_kernel(
    prop_hbm, obs_hbm, bucket_hbm, camp_ref, hour_ref, delay_ref,
    ga_ref, gb_ref, gc_ref,
    gb_sum, gc_sum, table_ref, obs_ref, bucket_ref, prop_ref, prop_sem, sems,
):
    parts = sems.shape[1]
    rows = obs_ref.shape[0] // parts

    def fetches(part):
        at = pl.ds(part * rows, rows)
        return (
            pltpu.make_async_copy(obs_hbm.at[at], obs_ref.at[at], sems.at[0, part]),
            pltpu.make_async_copy(bucket_hbm.at[at], bucket_ref.at[at], sems.at[1, part]),
        )

    def begin(part):
        if part < parts:
            for fetch in fetches(part):
                fetch.start()

    def arrived(part):
        begin(part + AHEAD)
        for fetch in fetches(part):
            fetch.wait()

    prop_fetch = pltpu.make_async_copy(prop_hbm, prop_ref, prop_sem)
    prop_fetch.start()
    for part in range(AHEAD):
        begin(part)
    prop_fetch.wait()
    fill_table(table_ref, prop_ref)
    tile_gradients(
        table_ref, obs_ref, bucket_ref, camp_ref, hour_ref, delay_ref,
        ga_ref, gb_ref, gc_ref, gb_sum, gc_sum, parts, arrived,
    )


def gradients(propensity, observed, bucket, camp_block, hour_block, delay_block):
    tile_rows, tile_cols, delay_count = observed.shape
    rank = camp_block.shape[1]
    parts = tile_rows // math.gcd(tile_rows, 16)
    vmem = pl.BlockSpec(memory_space=pltpu.VMEM)
    hbm = pl.BlockSpec(memory_space=pltpu.HBM)
    large = [pltpu.with_memory_space_constraint(x, pltpu.HBM) for x in (propensity, observed, bucket)]
    return pl.pallas_call(
        grads_kernel,
        in_specs=[hbm] * 3 + [vmem] * 3,
        out_specs=[vmem] * 3,
        out_shape=[
            jax.ShapeDtypeStruct((tile_rows, rank), F32),
            jax.ShapeDtypeStruct((tile_cols, rank), BF16),
            jax.ShapeDtypeStruct((delay_count, rank), BF16),
        ],
        scratch_shapes=[
            pltpu.VMEM((tile_cols, rank), F32),
            pltpu.VMEM((delay_count, rank), F32),
            pltpu.VMEM((8, delay_count), F32),
            pltpu.VMEM(observed.shape, observed.dtype),
            pltpu.VMEM(bucket.shape, bucket.dtype),
            pltpu.SMEM(propensity.shape, F32),
            pltpu.SemaphoreType.DMA,
            pltpu.SemaphoreType.DMA((2, parts)),
        ],
        compiler_params=pltpu.CompilerParams(vmem_limit_bytes=40 * 1024 * 1024),
        cost_estimate=pl.CostEstimate(
            flops=6 * tile_rows * tile_cols * delay_count * rank,
            bytes_accessed=6 * tile_rows * tile_cols * delay_count,
            transcendentals=0,
        ),
        name="gradients",
    )(*large, camp_block, hour_block, delay_block)


def pack_kernel(*refs):
    camp, hour, delay, camp_out, hour_out, delay_out = refs[:3], refs[3:6], refs[6], *refs[7:]
    for n in range(3):
        camp_out[n] = camp[n][...].astype(BF16)
        hour_out[n] = hour[n][...].astype(BF16)
    delay_out[...] = delay[...].astype(BF16)


def pack(camp, hour, delay):
    vmem = pl.BlockSpec(memory_space=pltpu.VMEM)
    arrays = [pltpu.with_memory_space_constraint(x, pltpu.HBM) for x in (*camp, *hour, delay)]
    return pl.pallas_call(
        pack_kernel,
        in_specs=[vmem] * 7,
        out_specs=[vmem] * 3,
        out_shape=[
            jax.ShapeDtypeStruct((3,) + camp[0].shape, BF16),
            jax.ShapeDtypeStruct((3,) + hour[0].shape, BF16),
            jax.ShapeDtypeStruct(delay.shape, BF16),
        ],
        compiler_params=pltpu.CompilerParams(vmem_limit_bytes=8 * 1024 * 1024),
        name="pack",
    )(*arrays)


def swap(block, axis, bit):
    size = lax.axis_size(axis)
    return lax.ppermute(block, axis, [(i, i ^ bit) for i in range(size)])


def bits_of(axis):
    size = lax.axis_size(axis)
    assert size & (size - 1) == 0
    return [1 << n for n in range(size.bit_length() - 1)]


def gather_blocks(block, axis):
    index = lax.axis_index(axis)
    for depth, bit in enumerate(reversed(bits_of(axis))):
        other = swap(block, axis, bit)
        high = (index & bit) != 0
        low_block = jnp.where(high, other, block)
        high_block = jnp.where(high, block, other)
        block = jnp.stack([low_block, high_block], axis=depth)
    count = lax.axis_size(axis)
    return block.reshape((count,) + block.shape[len(bits_of(axis)):])


def swap_both(block, camp_bit, hour_bit):
    hours = lax.axis_size("hour")
    size = lax.axis_size("camp") * hours
    return lax.ppermute(block, ("camp", "hour"), [(i, i ^ (camp_bit * hours + hour_bit)) for i in range(size)])


def add(*terms):
    terms = [t.astype(F32) for t in terms]
    while len(terms) > 1:
        terms = [terms[n] + terms[n + 1] for n in range(0, len(terms), 2)]
    return terms[0]


def rounded(block):
    return lax.optimization_barrier(block.astype(BF16))


class Rows:
    def __init__(self, block, axis, whole):
        self.axis, self.whole, self.bits = axis, whole, bits_of(axis)[::-1]
        self.block = block
        if not whole:
            rows, rank = block.shape
            own = rows >> len(self.bits)
            self.block = block.reshape((2,) * len(self.bits) + (own, rank))

    def send(self, bit):
        if self.whole:
            return self.block
        at = self.bits.index(bit)
        low, high = (lax.index_in_dim(self.block, n, at, keepdims=False) for n in (0, 1))
        is_high = (lax.axis_index(self.axis) & bit) != 0
        self.block = jnp.where(is_high, high, low)
        self.bits.remove(bit)
        return jnp.where(is_high, low, high)

    def receive(self, other):
        self.block = rounded(add(self.block, other))


def exchange(gradient, bit, extra):
    sent = gradient.send(bit)
    rank = sent.shape[-1]
    joint = jnp.concatenate([sent.reshape(-1, rank), extra])
    joint = swap(joint, gradient.axis, bit)
    gradient.receive(joint[:-extra.shape[0]].reshape(sent.shape))
    return joint[-extra.shape[0]:]


def sum_all(camp_grad, hour_grad, delay_grad, whole):
    camp_bits, hour_bits = bits_of("camp"), bits_of("hour")
    camp_rows = Rows(camp_grad.astype(BF16), "hour", whole)
    hour_rows = Rows(hour_grad, "camp", whole)
    first = camp_bits.pop(0)
    half = delay_grad.shape[0] // 2
    is_high = (lax.axis_index("camp") & first) != 0
    low, high = delay_grad[:half], delay_grad[half:]
    kept = jnp.where(is_high, high, low)
    delay_part = rounded(add(kept, exchange(hour_rows, first, jnp.where(is_high, low, high))))
    while camp_bits and hour_bits:
        camp_bit, hour_bit = camp_bits.pop(0), hour_bits.pop(0)
        other_camp = exchange(hour_rows, camp_bit, delay_part)
        other_hour = exchange(camp_rows, hour_bit, delay_part)
        other_both = swap_both(delay_part, camp_bit, hour_bit)
        delay_part = rounded(add(delay_part, other_hour, other_camp, other_both))
    for rows, bits in ((hour_rows, camp_bits), (camp_rows, hour_bits)):
        for bit in bits:
            delay_part = rounded(add(delay_part, exchange(rows, bit, delay_part)))
    other = swap(delay_part, "camp", first)
    delay_sum = jnp.concatenate([jnp.where(is_high, other, delay_part), jnp.where(is_high, delay_part, other)])
    return camp_rows.block.astype(F32), hour_rows.block.astype(F32), delay_sum.astype(F32)


def own_rows(block, axis, count):
    return lax.dynamic_slice_in_dim(block, lax.axis_index(axis) * count, count, 0)


def body(
    observed,
    bucket,
    propensity,
    camp_factor,
    camp_moment,
    camp_second,
    hour_factor,
    hour_moment,
    hour_second,
    delay_factor,
    delay_moment,
    delay_second,
):
    tile_rows, tile_cols, delay_count = observed.shape
    camp_own, hour_own = camp_factor.shape[0], hour_factor.shape[0]
    campaigns = tile_rows * lax.axis_size("camp")
    total_hours = tile_cols * lax.axis_size("hour")
    rank = camp_factor.shape[1]
    camp_scale = 1.0 / math.sqrt(total_hours * delay_count)
    hour_scale = 1.0 / math.sqrt(campaigns * delay_count)
    delay_scale = 1.0 / math.sqrt(campaigns * total_hours)

    camp_state = (camp_factor, camp_moment, camp_second)
    hour_state = (hour_factor, hour_moment, hour_second)
    camp_packed, hour_packed, delay_block = pack(camp_state, hour_state, delay_factor)
    camp_all = gather_blocks(camp_packed, "hour")
    hour_all = gather_blocks(hour_packed, "camp")
    camp_all = [camp_all[:, n].reshape(tile_rows, rank) for n in range(3)]
    hour_all = [hour_all[:, n].reshape(tile_cols, rank) for n in range(3)]
    camp_block, hour_block = camp_all[0], hour_all[0]

    partial = gradients(propensity, observed, bucket, camp_block, hour_block, delay_block)
    camp_grad, hour_grad, delay_grad = sum_all(*partial, whole=True)
    camp_block = adam_update(*(x.astype(F32) for x in camp_all), camp_grad, camp_scale)[0].astype(BF16)
    hour_block = adam_update(*(x.astype(F32) for x in hour_all), hour_grad, hour_scale)[0].astype(BF16)
    camp_state = adam_update(*camp_state, own_rows(camp_grad, "hour", camp_own), camp_scale)
    hour_state = adam_update(*hour_state, own_rows(hour_grad, "camp", hour_own), hour_scale)
    delay_state = adam_update(delay_factor, delay_moment, delay_second, delay_grad, delay_scale)
    delay_block = delay_state[0].astype(BF16)

    partial = gradients(propensity, observed, bucket, camp_block, hour_block, delay_block)
    camp_grad, hour_grad, delay_grad = sum_all(*partial, whole=False)
    camp_new = adam_update(*camp_state, camp_grad, camp_scale)[0]
    hour_new = adam_update(*hour_state, hour_grad, hour_scale)[0]
    delay_new = adam_update(*delay_state, delay_grad, delay_scale)[0]
    return (camp_new, hour_new, delay_new)


def solution(mesh):
    in_specs = (
        P("camp", "hour", None),
        P("camp", "hour", None),
        P(),
        P(("camp", "hour"), None),
        P(("camp", "hour"), None),
        P(("camp", "hour"), None),
        P(("hour", "camp"), None),
        P(("hour", "camp"), None),
        P(("hour", "camp"), None),
        P(),
        P(),
        P(),
    )
    out_specs = (P(("camp", "hour"), None), P(("hour", "camp"), None), P())
    return jax.shard_map(body, mesh=mesh, in_specs=in_specs, out_specs=out_specs, check_vma=False)
```

```python
import math

import jax
import jax.numpy as jnp
from jax import lax
from jax.experimental import pallas as pl
from jax.experimental.pallas import tpu as pltpu
from jax.sharding import PartitionSpec as P

learn_rate = 0.1
beta_first = 0.9
beta_second = 0.999
adam_eps = 1e-08

F32 = jnp.float32
BF16 = jnp.bfloat16


def adam_update(factor, moment, second, gradient, grad_scale):
    scaled = gradient * grad_scale
    moment = beta_first * moment + (1.0 - beta_first) * scaled
    second = beta_second * second + (1.0 - beta_second) * scaled * scaled
    factor = factor - learn_rate * moment / (jnp.sqrt(second) + adam_eps)
    return (factor, moment, second)


def fill_table(table_ref, prop_ref):
    lane = lax.broadcasted_iota(jnp.int32, table_ref.shape, 1)
    chance = jnp.ones(table_ref.shape, F32)
    for level in range(prop_ref.shape[0]):
        chance = jnp.where(lane == level + 1, prop_ref[level], chance)
    table_ref[...] = jnp.where(lane == 0, 0.0, 1.0 / chance)


def tile_gradients(
    table_ref, obs_ref, bucket_ref, camp_ref, hour_ref, delay_ref,
    ga_ref, gb_ref, gc_ref, gb_sum, gc_sum, cuts, arrived,
):
    cols, delays = obs_ref.shape[1:]
    rank = hour_ref.shape[1]
    sub = math.gcd(*cuts, 8)
    flat = sub * cols
    gb_sum[...] = jnp.zeros_like(gb_sum)
    gc_sum[...] = jnp.zeros_like(gc_sum)
    hour16 = hour_ref[...]
    hour = hour16.astype(F32)
    delay = delay_ref[...]
    for part in range(len(cuts) - 1):
        arrived(part)
        table = jnp.broadcast_to(table_ref[:1], (flat, delays))
        gb_part, gc_part = gb_sum[...], gc_sum[...]
        for start in range(cuts[part], cuts[part + 1], sub):
            camp = camp_ref[start:start + sub]
            pair = (camp[:, None, :] * hour16[None, :, :]).reshape(flat, rank)
            model = lax.dot_general(pair, delay, (((1,), (1,)), ((), ())), preferred_element_type=F32)
            bucket = bucket_ref[start:start + sub].reshape(flat, delays)
            weight = jnp.take_along_axis(table, bucket, axis=1)
            observed = obs_ref[start:start + sub].reshape(flat, delays).astype(F32)
            residual = (weight * (model - observed)).astype(BF16)
            back = jnp.dot(residual, delay, preferred_element_type=F32).reshape(sub, cols, rank)
            ga_ref[start:start + sub] = jnp.sum(back * hour[None, :, :], axis=1)
            gb_part += jnp.sum(back * camp.astype(F32)[:, None, :], axis=0)
            gc_part += lax.dot_general(residual, pair, (((0,), (0,)), ((), ())), preferred_element_type=F32)
        gb_sum[...] = gb_part
        gc_sum[...] = gc_part
    gb_ref[...] = gb_sum[...].astype(gb_ref.dtype)
    gc_ref[...] = gc_sum[...].astype(gc_ref.dtype)


AHEAD = 3
SHARES = (1, 1, 2, 4)


def cuts_of(rows):
    unit = rows // sum(SHARES)
    if unit * sum(SHARES) != rows or unit % 8:
        return (0, rows)
    return tuple(unit * sum(SHARES[:n]) for n in range(len(SHARES) + 1))


def grads_kernel(
    prop_hbm, obs_hbm, bucket_hbm, camp_ref, hour_ref, delay_ref,
    ga_ref, gb_ref, gc_ref,
    gb_sum, gc_sum, table_ref, obs_ref, bucket_ref, prop_ref, prop_sem, sems,
):
    cuts = cuts_of(obs_ref.shape[0])
    parts = len(cuts) - 1

    def fetches(part):
        at = pl.ds(cuts[part], cuts[part + 1] - cuts[part])
        return (
            pltpu.make_async_copy(obs_hbm.at[at], obs_ref.at[at], sems.at[0, part]),
            pltpu.make_async_copy(bucket_hbm.at[at], bucket_ref.at[at], sems.at[1, part]),
        )

    def begin(part):
        if part < parts:
            for fetch in fetches(part):
                fetch.start()

    def arrived(part):
        begin(part + AHEAD)
        for fetch in fetches(part):
            fetch.wait()

    prop_fetch = pltpu.make_async_copy(prop_hbm, prop_ref, prop_sem)
    prop_fetch.start()
    for part in range(AHEAD):
        begin(part)
    prop_fetch.wait()
    fill_table(table_ref, prop_ref)
    tile_gradients(
        table_ref, obs_ref, bucket_ref, camp_ref, hour_ref, delay_ref,
        ga_ref, gb_ref, gc_ref, gb_sum, gc_sum, cuts, arrived,
    )


def gradients(propensity, observed, bucket, camp_block, hour_block, delay_block):
    tile_rows, tile_cols, delay_count = observed.shape
    rank = camp_block.shape[1]
    parts = len(cuts_of(tile_rows)) - 1
    vmem = pl.BlockSpec(memory_space=pltpu.VMEM)
    hbm = pl.BlockSpec(memory_space=pltpu.HBM)
    large = [pltpu.with_memory_space_constraint(x, pltpu.HBM) for x in (propensity, observed, bucket)]
    return pl.pallas_call(
        grads_kernel,
        in_specs=[hbm] * 3 + [vmem] * 3,
        out_specs=[vmem] * 3,
        out_shape=[
            jax.ShapeDtypeStruct((tile_rows, rank), F32),
            jax.ShapeDtypeStruct((tile_cols, rank), BF16),
            jax.ShapeDtypeStruct((delay_count, rank), BF16),
        ],
        scratch_shapes=[
            pltpu.VMEM((tile_cols, rank), F32),
            pltpu.VMEM((delay_count, rank), F32),
            pltpu.VMEM((8, delay_count), F32),
            pltpu.VMEM(observed.shape, observed.dtype),
            pltpu.VMEM(bucket.shape, bucket.dtype),
            pltpu.SMEM(propensity.shape, F32),
            pltpu.SemaphoreType.DMA,
            pltpu.SemaphoreType.DMA((2, parts)),
        ],
        compiler_params=pltpu.CompilerParams(vmem_limit_bytes=40 * 1024 * 1024),
        cost_estimate=pl.CostEstimate(
            flops=6 * tile_rows * tile_cols * delay_count * rank,
            bytes_accessed=6 * tile_rows * tile_cols * delay_count,
            transcendentals=0,
        ),
        name="gradients",
    )(*large, camp_block, hour_block, delay_block)


def pack_kernel(*refs):
    camp, hour, delay, camp_out, hour_out, delay_out = refs[:3], refs[3:6], refs[6], *refs[7:]
    for n in range(3):
        camp_out[n] = camp[n][...].astype(BF16)
        hour_out[n] = hour[n][...].astype(BF16)
    delay_out[...] = delay[...].astype(BF16)


def pack(camp, hour, delay):
    vmem = pl.BlockSpec(memory_space=pltpu.VMEM)
    arrays = [pltpu.with_memory_space_constraint(x, pltpu.HBM) for x in (*camp, *hour, delay)]
    return pl.pallas_call(
        pack_kernel,
        in_specs=[vmem] * 7,
        out_specs=[vmem] * 3,
        out_shape=[
            jax.ShapeDtypeStruct((3,) + camp[0].shape, BF16),
            jax.ShapeDtypeStruct((3,) + hour[0].shape, BF16),
            jax.ShapeDtypeStruct(delay.shape, BF16),
        ],
        compiler_params=pltpu.CompilerParams(vmem_limit_bytes=8 * 1024 * 1024),
        name="pack",
    )(*arrays)


def swap(block, axis, bit):
    size = lax.axis_size(axis)
    return lax.ppermute(block, axis, [(i, i ^ bit) for i in range(size)])


def bits_of(axis):
    size = lax.axis_size(axis)
    assert size & (size - 1) == 0
    return [1 << n for n in range(size.bit_length() - 1)]


def gather_blocks(block, axis):
    index = lax.axis_index(axis)
    for depth, bit in enumerate(reversed(bits_of(axis))):
        other = swap(block, axis, bit)
        high = (index & bit) != 0
        low_block = jnp.where(high, other, block)
        high_block = jnp.where(high, block, other)
        block = jnp.stack([low_block, high_block], axis=depth)
    count = lax.axis_size(axis)
    return block.reshape((count,) + block.shape[len(bits_of(axis)):])


def swap_both(block, camp_bit, hour_bit):
    hours = lax.axis_size("hour")
    size = lax.axis_size("camp") * hours
    return lax.ppermute(block, ("camp", "hour"), [(i, i ^ (camp_bit * hours + hour_bit)) for i in range(size)])


def add(*terms):
    terms = [t.astype(F32) for t in terms]
    while len(terms) > 1:
        terms = [terms[n] + terms[n + 1] for n in range(0, len(terms), 2)]
    return terms[0]


def rounded(block):
    return lax.optimization_barrier(block.astype(BF16))


class Rows:
    def __init__(self, block, axis, whole):
        self.axis, self.whole, self.bits = axis, whole, bits_of(axis)[::-1]
        self.block = block
        if not whole:
            rows, rank = block.shape
            own = rows >> len(self.bits)
            self.block = block.reshape((2,) * len(self.bits) + (own, rank))

    def send(self, bit):
        if self.whole:
            return self.block
        at = self.bits.index(bit)
        low, high = (lax.index_in_dim(self.block, n, at, keepdims=False) for n in (0, 1))
        is_high = (lax.axis_index(self.axis) & bit) != 0
        self.block = jnp.where(is_high, high, low)
        self.bits.remove(bit)
        return jnp.where(is_high, low, high)

    def receive(self, other):
        self.block = rounded(add(self.block, other))


def exchange(gradient, bit, extra):
    sent = gradient.send(bit)
    rank = sent.shape[-1]
    joint = jnp.concatenate([sent.reshape(-1, rank), extra])
    joint = swap(joint, gradient.axis, bit)
    gradient.receive(joint[:-extra.shape[0]].reshape(sent.shape))
    return joint[-extra.shape[0]:]


def sum_all(camp_grad, hour_grad, delay_grad, whole):
    camp_bits, hour_bits = bits_of("camp"), bits_of("hour")
    camp_rows = Rows(camp_grad.astype(BF16), "hour", whole)
    hour_rows = Rows(hour_grad, "camp", whole)
    first = camp_bits.pop(0)
    half = delay_grad.shape[0] // 2
    is_high = (lax.axis_index("camp") & first) != 0
    low, high = delay_grad[:half], delay_grad[half:]
    kept = jnp.where(is_high, high, low)
    delay_part = rounded(add(kept, exchange(hour_rows, first, jnp.where(is_high, low, high))))
    while camp_bits and hour_bits:
        camp_bit, hour_bit = camp_bits.pop(0), hour_bits.pop(0)
        other_camp = exchange(hour_rows, camp_bit, delay_part)
        other_hour = exchange(camp_rows, hour_bit, delay_part)
        other_both = swap_both(delay_part, camp_bit, hour_bit)
        delay_part = rounded(add(delay_part, other_hour, other_camp, other_both))
    for rows, bits in ((hour_rows, camp_bits), (camp_rows, hour_bits)):
        for bit in bits:
            delay_part = rounded(add(delay_part, exchange(rows, bit, delay_part)))
    other = swap(delay_part, "camp", first)
    delay_sum = jnp.concatenate([jnp.where(is_high, other, delay_part), jnp.where(is_high, delay_part, other)])
    return camp_rows.block.astype(F32), hour_rows.block.astype(F32), delay_sum.astype(F32)


def own_rows(block, axis, count):
    return lax.dynamic_slice_in_dim(block, lax.axis_index(axis) * count, count, 0)


def body(
    observed,
    bucket,
    propensity,
    camp_factor,
    camp_moment,
    camp_second,
    hour_factor,
    hour_moment,
    hour_second,
    delay_factor,
    delay_moment,
    delay_second,
):
    tile_rows, tile_cols, delay_count = observed.shape
    camp_own, hour_own = camp_factor.shape[0], hour_factor.shape[0]
    campaigns = tile_rows * lax.axis_size("camp")
    total_hours = tile_cols * lax.axis_size("hour")
    rank = camp_factor.shape[1]
    camp_scale = 1.0 / math.sqrt(total_hours * delay_count)
    hour_scale = 1.0 / math.sqrt(campaigns * delay_count)
    delay_scale = 1.0 / math.sqrt(campaigns * total_hours)

    camp_state = (camp_factor, camp_moment, camp_second)
    hour_state = (hour_factor, hour_moment, hour_second)
    camp_packed, hour_packed, delay_block = pack(camp_state, hour_state, delay_factor)
    camp_all = gather_blocks(camp_packed, "hour")
    hour_all = gather_blocks(hour_packed, "camp")
    camp_all = [camp_all[:, n].reshape(tile_rows, rank) for n in range(3)]
    hour_all = [hour_all[:, n].reshape(tile_cols, rank) for n in range(3)]
    camp_block, hour_block = camp_all[0], hour_all[0]

    partial = gradients(propensity, observed, bucket, camp_block, hour_block, delay_block)
    camp_grad, hour_grad, delay_grad = sum_all(*partial, whole=True)
    camp_block = adam_update(*(x.astype(F32) for x in camp_all), camp_grad, camp_scale)[0].astype(BF16)
    hour_block = adam_update(*(x.astype(F32) for x in hour_all), hour_grad, hour_scale)[0].astype(BF16)
    camp_state = adam_update(*camp_state, own_rows(camp_grad, "hour", camp_own), camp_scale)
    hour_state = adam_update(*hour_state, own_rows(hour_grad, "camp", hour_own), hour_scale)
    delay_state = adam_update(delay_factor, delay_moment, delay_second, delay_grad, delay_scale)
    delay_block = delay_state[0].astype(BF16)

    partial = gradients(propensity, observed, bucket, camp_block, hour_block, delay_block)
    camp_grad, hour_grad, delay_grad = sum_all(*partial, whole=False)
    camp_new = adam_update(*camp_state, camp_grad, camp_scale)[0]
    hour_new = adam_update(*hour_state, hour_grad, hour_scale)[0]
    delay_new = adam_update(*delay_state, delay_grad, delay_scale)[0]
    return (camp_new, hour_new, delay_new)


def solution(mesh):
    in_specs = (
        P("camp", "hour", None),
        P("camp", "hour", None),
        P(),
        P(("camp", "hour"), None),
        P(("camp", "hour"), None),
        P(("camp", "hour"), None),
        P(("hour", "camp"), None),
        P(("hour", "camp"), None),
        P(("hour", "camp"), None),
        P(),
        P(),
        P(),
    )
    out_specs = (P(("camp", "hour"), None), P(("hour", "camp"), None), P())
    return jax.shard_map(body, mesh=mesh, in_specs=in_specs, out_specs=out_specs, check_vma=False)
```
